32 devices in a mesh: lists: 8 (over z, x), help: 4 (over y, core).
Axes of the slice: x: 2, y: 2, z: 4, core: 2. Of those that a mesh axis runs over, the one named last changes fastest.
Arguments:
- vectors: float32 [16, 1024, 768], P('lists', 'help'), may hold values from -6 to 6
- labels: int32 [16, 1024], P('lists', 'help'), may hold values from 0 to 1, as said below
- list_sizes: int32 [16], P('lists'), may hold values from 64 to 1024, as said below
- centroids: float32 [16, 768], P('lists'), may hold values from -4 to 4
- split_ids: int32 [4], replicated, may hold values from 0 to 15, as said below
- nearby: int32 [4, 8], replicated, may hold values from 0 to 15, as said below
- owner_map: int32 [16], replicated, may hold values from 0 to 15, as said below
- mover_source: int32 [4096], P(('lists', 'help')), may hold values from 0 to 511, as said below
- mover_dest: int32 [4096], P(('lists', 'help')), may hold values from -1 to 15, as said below
Outputs:
- gains: float32 [16, 1024], P('lists', 'help')
- arrivals: float32 [16, 512, 768], P('lists')
The draws below stay inside these ranges and needn't reach their ends.
Inputs may be any that keep to these rules, and one draw needn't show every extreme that they name: `split_ids`: distinct list ids. `nearby`: for each split, 8 distinct list ids, none equal to the split list. `owner_map`: a permutation of the slots. `list_sizes`: every list has at least two live rows; every split list has at least 576 live rows; the first slot of every index of lists that does not hold a split list holds at least 832 live rows. `labels`: row 0 of every list has label 0 and row 1 label 1. `mover_source`: distinct rows of the source device's block, live ones first. `mover_dest`: -1 exactly where the mover's source row is not live; from one device at most 32 live movers go to lists stored on one index of lists; every list slot receives at most 512 rows in all. Numbers of movers counted from these ids (per device and slot, or running totals of them) are small exact integers and may cross devices in any exact integer encoding, several to a word.
All inputs are finite; a program needn't handle non-finite values.
Results may differ from the reference program's by a relative error of at most 0.0003.
Values sent between devices are 32-bit elements; how exact they have to be, the bound alone decides.
A program may use at most 64 MiB of HBM per device.

```python
import jax
import jax.numpy as jnp
from jax import lax

D = 768
LIST_DEV = 2
CAP = 1024
NEAR = 8
MOVE_DEV = 128
NLISTS = 16
SPLITS = 4
MOVERS = 4096
MOST = 32
ARRIVE_CAP = 512
N_HELP = 4


def layout(key):
    keys = jax.random.split(jax.random.fold_in(key, 7), 8)
    lists_count = NLISTS // LIST_DEV
    sources = MOVERS // MOVE_DEV
    help_count = sources // lists_count
    rows = CAP // help_count
    local = LIST_DEV * rows
    order = jax.random.permutation(keys[0], NLISTS).astype(jnp.int32)
    split_ids = order[:SPLITS]

    def near_one(k):
        return jax.random.permutation(k, NLISTS - 1)[:NEAR].astype(jnp.int32) + 1
    offsets = jax.vmap(near_one)(jax.random.split(keys[1], SPLITS))
    nearby = (split_ids[:, None] + offsets) % NLISTS
    owner = jax.random.permutation(keys[2], NLISTS).astype(jnp.int32)
    slot_list = jnp.argsort(owner).astype(jnp.int32)
    flagged = jnp.zeros((NLISTS,), jnp.int32).at[split_ids].set(1)[slot_list]
    lower = jax.random.randint(keys[3], (NLISTS,), CAP // 16, 3 * CAP // 8 + 1)
    upper = jax.random.randint(keys[4], (NLISTS,), 9 * CAP // 16, CAP + 1)
    full = jax.random.randint(keys[7], (NLISTS,), 13 * CAP // 16, CAP + 1)
    leading_slot = jnp.arange(NLISTS, dtype=jnp.int32) % LIST_DEV == 0
    sizes = jnp.where(flagged == 1, upper, jnp.where(leading_slot, full, lower))
    sizes = sizes.astype(jnp.int32).at[owner[split_ids[0]]].set(CAP)
    hottest = jax.random.randint(keys[5], (), 0, lists_count)

    def movers_of(k, device):
        ka, kb = jax.random.split(k, 2)
        lists_part = device // help_count
        help_part = device % help_count
        mine = jnp.arange(local, dtype=jnp.int32)
        slot = lists_part * LIST_DEV + mine // rows
        alive = help_part * rows + mine % rows < sizes[slot]
        live_count = jnp.sum(alive.astype(jnp.int32))
        shuffled = jax.random.permutation(ka, local).astype(jnp.int32)
        ranking = jnp.zeros((local,), jnp.int32).at[shuffled].set(mine)
        scores = jnp.where(alive, 0, local) + ranking
        source = jnp.argsort(scores)[:MOVE_DEV].astype(jnp.int32)
        tokens = jax.random.permutation(kb, lists_count * MOST).astype(jnp.int32)
        leading = jnp.argsort(jnp.where(tokens // MOST == hottest, 0, 1), stable=True)
        picked = tokens[leading][:MOVE_DEV]
        target = picked // MOST
        within = picked % MOST % LIST_DEV
        dest = slot_list[target * LIST_DEV + within]
        dest = jnp.where(jnp.arange(MOVE_DEV, dtype=jnp.int32) < live_count, dest, -1).astype(jnp.int32)
        return (source, dest)
    source_all, dest_all = jax.vmap(movers_of)(jax.random.split(keys[6], sources), jnp.arange(sources, dtype=jnp.int32))
    return (split_ids, nearby, owner, sizes, source_all.reshape(-1), dest_all.reshape(-1))


def draw_split_ids(key, part):
    return layout(key)[0]


def draw_nearby(key, part):
    return layout(key)[1]


def draw_owner_map(key, part):
    return layout(key)[2]


def draw_list_sizes(key, part):
    return layout(key)[3]


def draw_mover_source(key, part):
    return layout(key)[4]


def draw_mover_dest(key, part):
    return layout(key)[5]


def draw_labels(key, part):
    coins = jax.random.randint(jax.random.fold_in(key, 11), (NLISTS, CAP), 0, 2)
    return coins.at[:, 0].set(0).at[:, 1].set(1).astype(jnp.int32)


def draw_vectors(key, part):
    ka, kb = jax.random.split(jax.random.fold_in(key, 13), 2)
    centre = jax.random.normal(ka, (NLISTS, 1, D), jnp.float32) * 0.7
    value = centre + 0.5 * jax.random.normal(kb, (NLISTS, CAP, D), jnp.float32)
    return jnp.clip(value, -6.0, 6.0).astype(jnp.float32)


def shard_levels(key, extent, cuts, least, high):
    level, own = 1.0, jax.random.fold_in(key, 6)
    for axis_at, blocks in cuts:
        draws = jnp.exp(jax.random.uniform(jax.random.fold_in(own, axis_at), (blocks,), jnp.float32, least / len(cuts), high / len(cuts)))
        level = level * jnp.repeat(draws, extent[axis_at] // blocks).reshape([-1 if axis == axis_at else 1 for axis in range(len(extent))])
    return level


def bell_draw(key, dims, scale, most, shards=(), kind=jnp.bfloat16):
    gain = shard_levels(key, dims, shards, -0.22, 0.18) if shards else 1.0
    entries = jax.random.normal(key, dims, jnp.float32) * scale * gain
    return jnp.minimum(jnp.maximum(entries, -most), most).astype(kind)


def setup_inputs(seed: int = 0) -> dict:
    splits = jax.random.split(jax.random.key(seed), 10)
    vectors = draw_vectors(jax.random.fold_in(splits[9], 71), 0)
    labels = draw_labels(jax.random.fold_in(splits[9], 71), 0)
    list_sizes = draw_list_sizes(jax.random.fold_in(splits[9], 71), 0)
    centroids = bell_draw(splits[3], (NLISTS, D), 0.7, 4.0, ((0, 8),), jnp.float32)
    split_ids = draw_split_ids(jax.random.fold_in(splits[9], 71), 0)
    nearby = draw_nearby(jax.random.fold_in(splits[9], 71), 0)
    owner_map = draw_owner_map(jax.random.fold_in(splits[9], 71), 0)
    mover_source = draw_mover_source(jax.random.fold_in(splits[9], 71), 0)
    mover_dest = draw_mover_dest(jax.random.fold_in(splits[9], 71), 0)
    return dict(vectors=vectors, labels=labels, list_sizes=list_sizes, centroids=centroids, split_ids=split_ids, nearby=nearby, owner_map=owner_map, mover_source=mover_source, mover_dest=mover_dest)


HIGH = lax.Precision.HIGHEST


def reference(vectors, labels, list_sizes, centroids, split_ids, nearby, owner_map, mover_source, mover_dest):
    total, cap, width = vectors.shape
    rows_index = jnp.arange(cap, dtype=jnp.int32)
    valid = rows_index[None, :] < list_sizes[:, None]
    split_slots = owner_map[split_ids]
    chosen = vectors[split_slots]
    chosen_labels = labels[split_slots]
    chosen_valid = valid[split_slots]
    halves = jnp.stack([(chosen_labels == 0) & chosen_valid, (chosen_labels == 1) & chosen_valid], axis=1).astype(jnp.float32)
    sums = jnp.einsum("sac,scd->sad", halves, chosen, precision=HIGH)
    counts = jnp.sum(halves, axis=2)
    new_cent = sums / counts[:, :, None]
    cents = new_cent.reshape(-1, width)
    sq_cent = jnp.sum(cents * cents, axis=1)
    near_slots = owner_map[nearby]
    slot_ids = jnp.arange(total, dtype=jnp.int32)
    hit = jnp.any(near_slots[None, :, :] == slot_ids[:, None, None], axis=2)

    def score(args):
        block, cent, mask, okay = args
        square = jnp.sum(block * block, axis=1)
        cross = jnp.dot(block, cents.T, precision=HIGH)
        dist = square[:, None] - 2.0 * cross + sq_cent[None, :]
        far = jnp.min(jnp.where(jnp.repeat(mask, 2)[None, :], dist, 1e30), axis=1)
        own = square - 2.0 * jnp.dot(block, cent, precision=HIGH) + jnp.sum(cent * cent)
        return jnp.where(okay & jnp.any(mask), (own - far) / width, 0.0)

    gains = lax.map(score, (vectors, centroids, hit, valid))
    rows = cap // N_HELP
    count = mover_source.shape[0]
    device = jnp.arange(count, dtype=jnp.int32) // MOVE_DEV
    lists_part = device // N_HELP
    help_part = device % N_HELP
    slot = lists_part * LIST_DEV + mover_source // rows
    row = help_part * rows + mover_source % rows
    moving = vectors[slot, row]
    live_move = mover_dest >= 0
    dest = jnp.where(live_move, owner_map[jnp.maximum(mover_dest, 0)], total).astype(jnp.int32)
    order = jnp.argsort(dest, stable=True).astype(jnp.int32)
    sorted_dest = dest[order]
    starts = jnp.searchsorted(sorted_dest, jnp.arange(total + 1, dtype=jnp.int32)).astype(jnp.int32)
    rank_sorted = jnp.arange(count, dtype=jnp.int32) - starts[sorted_dest]
    position = jnp.zeros((count,), jnp.int32).at[order].set(rank_sorted)
    place = jnp.where(live_move, dest * ARRIVE_CAP + position, total * ARRIVE_CAP).astype(jnp.int32)
    arrivals = jnp.zeros((total * ARRIVE_CAP, width), jnp.float32).at[place].set(moving, mode="drop")
    return gains, arrivals.reshape(total, ARRIVE_CAP, width)
```

```python
import functools

import jax
import jax.numpy as jnp
from jax import lax
from jax.experimental import pallas as pl
from jax.experimental.pallas import tpu as pltpu
from jax.sharding import PartitionSpec as P

MESH = pl.DeviceIdType.MESH
F32 = jnp.float32
BF16 = jnp.bfloat16


def split_parts(x):
    hi = x.astype(BF16)
    return hi, (x - hi.astype(F32)).astype(BF16)


def dot(a, b):
    return lax.dot_general(a, b, (((1,), (0,)), ((), ())), preferred_element_type=F32)


def dot_t(a, b):
    return lax.dot_general(a, b, (((1,), (1,)), ((), ())), preferred_element_type=F32)


def iota(shape, axis):
    return lax.broadcasted_iota(jnp.int32, shape, axis)


def kernel(
    lists, helps, depth, cap, crows,
    vec, labels, cent, msrc, mdst, sizes, split_ids, nearby, owner,
    gains, out,
    vhi, vlo, buckets, recv, flag_out, flags, flag_mat, codes, parts, cents, table,
    s_flag, r_flag, s_fgat, r_fgat, s_bkt, r_bkt, s_core, r_core, s_y, r_y, s_rel, r_rel,
    s_part, r_part, s_cent, r_cent,
):
    me = lax.axis_index("lists")
    hp = lax.axis_index("help")
    list_dev, rows, width = vec.shape
    n_rows = list_dev * rows
    moves = mdst.shape[1]
    n_splits, near = nearby.shape
    total_lists = owner.shape[0]
    first = me * list_dev
    core = lax.rem(hp, 2) * -2 + 1 + hp
    far = lax.rem(hp + 2, 4)
    diag = lax.rem(core + 2, 4)

    barrier = pltpu.get_barrier_semaphore()

    def greet(d, c):
        pl.semaphore_signal(
            barrier, inc=1, device_id=(lax.rem(me + d, lists), hp), device_id_type=MESH
        )
        return c

    lax.fori_loop(1, lists, greet, 0)
    for d in range(1, helps):
        pl.semaphore_signal(
            barrier, inc=1, device_id=(me, lax.rem(hp + d, helps)), device_id_type=MESH
        )

    hi, lo = split_parts(vec[...].reshape(n_rows, width))
    vhi[...] = hi
    vlo[...] = lo

    lane = iota((crows, n_rows), 1)
    row = iota((crows, n_rows), 0)
    label = jnp.concatenate([labels[k : k + 1, :] for k in range(list_dev)], axis=1)
    limit = jnp.zeros((1, n_rows), jnp.int32)
    lane1 = iota((1, n_rows), 1)
    for k in range(list_dev):
        inside = (lane1 >= k * rows) & (lane1 < (k + 1) * rows)
        limit = jnp.where(inside, sizes[k] + k * rows - hp * rows, limit)
    live_label = jnp.where(lane1 < limit, label, -1)
    half = jnp.zeros((crows, n_rows), F32)
    for k in range(list_dev):
        for a in range(2):
            pick = (row == 2 * k + a) & (lane >= k * rows) & (lane < (k + 1) * rows)
            half = jnp.where(pick & (live_label == a), 1.0, half)
    hb = half.astype(BF16)
    mine = dot(hb, hi) + dot(hb, lo)
    number = jnp.sum(half, axis=1, keepdims=True)
    parts[hp, :, 0:width] = mine
    parts[hp, :, width:] = jnp.broadcast_to(number, (crows, 128))

    dest = mdst[...]
    slot = jnp.full((1, moves), -1, jnp.int32)
    for x in range(total_lists):
        slot = jnp.where(dest == x, owner[x], slot)
    alive = slot >= 0
    slot_f = slot.astype(F32)
    peer = jnp.where(alive, jnp.floor(slot_f / list_dev), -1.0)
    local = jnp.where(alive, slot_f - peer * list_dev + 1.0, 0.0)
    peer_is = peer == iota((lists, moves), 0).astype(F32)
    peers = jnp.where(peer_is, 1.0, 0.0)
    upper = jnp.where(iota((moves, moves), 0) < iota((moves, moves), 1), 1.0, 0.0).astype(BF16)
    rank = jnp.sum(dot(peers.astype(BF16), upper) * peers, axis=0, keepdims=True)
    at = jnp.where(alive, peer * depth + rank, -1.0).astype(jnp.int32)
    chosen = jnp.where(at == iota((lists * depth, moves), 0), 1.0, 0.0).astype(BF16)
    source = jnp.where(msrc[...] == iota((n_rows, moves), 0), 1.0, 0.0).astype(BF16)
    gather = dot_t(chosen, source).astype(BF16)
    buckets[...] = (dot(gather, hi) + dot(gather, lo)).reshape(lists, depth, width)
    ranked = jnp.where(
        jnp.where(alive, rank, -1.0).astype(jnp.int32) == iota((128, moves), 0), 1.0, 0.0
    ).astype(BF16)
    flag_rows = dot_t(jnp.where(peer_is, local, 0.0).astype(BF16), ranked)
    for p in range(lists):
        flag_out[p] = flag_rows[p : p + 1, :]

    pl.semaphore_wait(barrier, lists - 1 + helps - 1)

    def flag_copy(d):
        return pltpu.make_async_remote_copy(
            src_ref=flag_out.at[lax.rem(me + d, lists)],
            dst_ref=flags.at[hp, me],
            send_sem=s_flag.at[d], recv_sem=r_flag.at[d],
            device_id=(lax.rem(me + d, lists), hp), device_id_type=MESH,
        )

    def bucket_copy(d):
        return pltpu.make_async_remote_copy(
            src_ref=buckets.at[lax.rem(me + d, lists)],
            dst_ref=recv.at[me, hp],
            send_sem=s_bkt.at[d], recv_sem=r_bkt.at[d],
            device_id=(lax.rem(me + d, lists), hp), device_id_type=MESH,
        )

    def cent_copy(d):
        return pltpu.make_async_remote_copy(
            src_ref=cents.at[me], dst_ref=cents.at[me],
            send_sem=s_cent.at[d], recv_sem=r_cent.at[d],
            device_id=(lax.rem(me + d, lists), hp), device_id_type=MESH,
        )

    def help_copy(ref, sends, recvs, d):
        return pltpu.make_async_remote_copy(
            src_ref=ref.at[hp], dst_ref=ref.at[hp],
            send_sem=sends.at[d], recv_sem=recvs.at[d],
            device_id=(me, lax.rem(hp + d, helps)), device_id_type=MESH,
        )

    def piece_copy(d, owner_h, target, sends, recvs):
        piece = recv.at[lax.rem(me + lists - d, lists), owner_h]
        return pltpu.make_async_remote_copy(
            src_ref=piece, dst_ref=piece,
            send_sem=sends.at[d], recv_sem=recvs.at[d],
            device_id=(me, target), device_id_type=MESH,
        )

    def to_core(d):
        return piece_copy(d, hp, core, s_core, r_core)

    def to_far(d):
        return piece_copy(d, hp, far, s_y, r_y)

    def relay(d):
        return piece_copy(d, far, core, s_rel, r_rel)

    for d in range(1, helps):
        help_copy(parts, s_part, r_part, d).start()

    def each(lower, upper_, fn):
        def body(d, c):
            fn(d)
            return c

        lax.fori_loop(lower, upper_, body, 0)

    each(1, lists, lambda d: flag_copy(d).start())
    each(1, lists, lambda d: bucket_copy(d).start())
    recv[me, hp] = buckets[me]
    flags[hp, me] = flag_out[me]
    to_core(0).start()
    to_far(0).start()

    for d in range(1, helps):
        help_copy(parts, s_part, r_part, d).wait_recv()
    summed = parts[0]
    for h in range(1, helps):
        summed = summed + parts[h]
    new_c = summed[:, 0:width] / jnp.maximum(summed[:, width : width + 1], 1.0)
    cents[me] = new_c
    each(1, lists, lambda d: cent_copy(d).start())

    each(1, lists, lambda d: flag_copy(d).wait_recv())
    for d in range(1, helps):
        help_copy(flags, s_fgat, r_fgat, d).start()
    for d in range(1, helps):
        help_copy(flags, s_fgat, r_fgat, d).wait_recv()
    for x in range(lists):
        for h in range(helps):
            flag_mat[x * helps + h : x * helps + h + 1, :] = flags[h, x]
    sources = lists * helps
    flag = flag_mat[...]
    before_lane = jnp.where(iota((128, 128), 0) < iota((128, 128), 1), 1.0, 0.0).astype(BF16)
    before_row = jnp.where(
        iota((sources, sources), 0) > iota((sources, sources), 1), 1.0, 0.0
    ).astype(BF16)
    ones = jnp.ones((128, 128), BF16)
    code = jnp.full((sources, 128), -1.0, F32)
    for k in range(list_dev):
        is_k = flag == float(k + 1)
        one_k = jnp.where(is_k, 1.0, 0.0).astype(BF16)
        place = dot(one_k, before_lane) + dot(before_row, dot(one_k, ones).astype(BF16))
        code = jnp.where(is_k, place + float(k * cap), code)
    spread = jnp.where(iota((sources, 128), 1) < depth, code, 0.0)
    step = depth
    while step < 128:
        spread = spread + pltpu.roll(spread, step, 1)
        step *= 2
    lane_h = iota((sources, 128), 1)
    row_h = lax.rem(iota((sources, 128), 0), helps)
    spread = jnp.where((lane_h >= row_h * depth) & (lane_h < (row_h + 1) * depth), spread, 0.0)
    for x in range(lists):
        codes[x] = jnp.sum(spread[x * helps : (x + 1) * helps, :], axis=0, keepdims=True)

    def ready(d):
        @pl.when(d > 0)
        def _():
            bucket_copy(d).wait_recv()
            to_core(d).start()
            to_far(d).start()

    def pass_on(d):
        to_far(d).wait_recv()
        relay(d).start()

    taken = helps * depth

    def place_piece(d, fresh):
        to_core(d).wait_recv()
        relay(d).wait_recv()
        x = lax.rem(me + lists - d, lists)
        put = codes[x][:, 0:taken].astype(jnp.int32)
        onehot = jnp.where(put == iota((list_dev * cap, taken), 0), 1.0, 0.0).astype(BF16)
        a, b = split_parts(recv[x].reshape(taken, width))
        moved = dot(onehot, a) + dot(onehot, b)
        if fresh:
            out[...] = moved.reshape(list_dev, cap, width)
        else:
            out[...] += moved.reshape(list_dev, cap, width)

    def turn(d):
        ready(d)
        pass_on(d - 1)
        place_piece(d - 2, False)

    ready(1)
    pass_on(0)
    ready(2)
    pass_on(1)
    place_piece(0, True)
    each(3, lists, turn)

    each(1, lists, lambda d: cent_copy(d).wait_recv())
    n_c = lists * crows
    table[0:n_c, :] = cents[...].reshape(n_c, width)
    table[n_c:, :] = jnp.zeros((crows, width), F32)
    for k in range(list_dev):
        table[n_c + k : n_c + k + 1, :] = cent[k : k + 1, :]
    every = table[...]
    c_hi, c_lo = split_parts(every)
    cross = dot_t(c_hi, vhi[...]) + dot_t(c_hi, vlo[...]) + dot_t(c_lo, vhi[...])
    score = jnp.sum(every * every, axis=1, keepdims=True) - 2.0 * cross
    c_row = iota((n_c, rows), 0)
    in_block = lax.rem(c_row, crows)
    slot_of = jnp.where(
        in_block < 2 * list_dev,
        lax.div(c_row, crows) * list_dev + lax.div(in_block, 2),
        -1,
    )
    for k in range(list_dev):
        seen = jnp.zeros((n_c, rows), jnp.int32)
        touched = jnp.int32(0)
        for s in range(n_splits):
            at_slot = owner[split_ids[s]]
            hit = jnp.int32(0)
            for n in range(near):
                hit = jnp.maximum(
                    hit, jnp.where(owner[nearby[s, n]] == first + k, 1, 0).astype(jnp.int32)
                )
            touched = jnp.maximum(touched, hit)
            seen = jnp.maximum(seen, jnp.where(slot_of == at_slot, hit, 0))
        block = score[:, k * rows : (k + 1) * rows]
        best = jnp.min(jnp.where(seen > 0, block[0:n_c], 1e30), axis=0, keepdims=True)
        own = block[n_c + k : n_c + k + 1, :]
        top = jnp.where(touched > 0, sizes[k] - hp * rows, 0)
        ok = iota((1, rows), 1) < top
        gains[k : k + 1, :] = jnp.where(ok, (own - best) * (1.0 / width), 0.0)

    pass_on(lists - 1)
    place_piece(lists - 2, False)
    place_piece(lists - 1, False)

    def drain(d):
        flag_copy(d).wait_send()
        bucket_copy(d).wait_send()
        cent_copy(d).wait_send()

    each(1, lists, drain)

    def drain_pieces(d):
        to_core(d).wait_send()
        to_far(d).wait_send()
        relay(d).wait_send()

    each(0, lists, drain_pieces)
    for d in range(1, helps):
        help_copy(parts, s_part, r_part, d).wait_send()
        help_copy(flags, s_fgat, r_fgat, d).wait_send()


def local(
    vectors, labels, list_sizes, centroids, split_ids, nearby, owner_map, mover_source, mover_dest
):
    list_dev, rows, width = vectors.shape
    lists = lax.axis_size("lists")
    helps = lax.axis_size("help")
    moves = mover_source.shape[0]
    most = max(2, (moves + lists - 1) // lists * 2)
    cap = lists * helps * ((most + list_dev - 1) // list_dev)
    depth = (most + 7) // 8 * 8
    crows = (2 * list_dev + 7) // 8 * 8
    vm = pl.BlockSpec(memory_space=pltpu.VMEM)
    sm = pl.BlockSpec(memory_space=pltpu.SMEM)
    sem = pltpu.SemaphoreType.DMA
    gains, arrived = pl.pallas_call(
        functools.partial(kernel, lists, helps, depth, cap, crows),
        out_shape=(
            jax.ShapeDtypeStruct((list_dev, rows), F32),
            jax.ShapeDtypeStruct((list_dev, cap, width), F32),
        ),
        in_specs=[vm] * 5 + [sm] * 4,
        out_specs=(vm, vm),
        scratch_shapes=[
            pltpu.VMEM((list_dev * rows, width), BF16),
            pltpu.VMEM((list_dev * rows, width), BF16),
            pltpu.VMEM((lists, depth, width), F32),
            pltpu.VMEM((lists, helps, depth, width), F32),
            pltpu.VMEM((lists, 1, 128), F32),
            pltpu.VMEM((helps, lists, 1, 128), F32),
            pltpu.VMEM((lists * helps, 128), F32),
            pltpu.VMEM((lists, 1, 128), F32),
            pltpu.VMEM((helps, crows, width + 128), F32),
            pltpu.VMEM((lists, crows, width), F32),
            pltpu.VMEM((lists * crows + crows, width), F32),
            sem((lists,)), sem((lists,)), sem((helps,)), sem((helps,)),
            sem((lists,)), sem((lists,)), sem((lists,)), sem((lists,)),
            sem((lists,)), sem((lists,)), sem((lists,)), sem((lists,)),
            sem((helps,)), sem((helps,)), sem((lists,)), sem((lists,)),
        ],
        compiler_params=pltpu.CompilerParams(
            collective_id=0, has_side_effects=True, vmem_limit_bytes=56 * 1024 * 1024
        ),
    )(
        vectors, labels, centroids, mover_source.reshape(1, moves), mover_dest.reshape(1, moves),
        list_sizes, split_ids, nearby, owner_map,
    )
    return gains, arrived


def solution(mesh):
    in_specs = (
        P("lists", "help", None),
        P("lists", "help"),
        P("lists"),
        P("lists", None),
        P(),
        P(),
        P(),
        P(("lists", "help")),
        P(("lists", "help")),
    )
    out_specs = (P("lists", "help"), P("lists", None, None))
    return jax.shard_map(local, mesh=mesh, in_specs=in_specs, out_specs=out_specs, check_vma=False)
```

```python
import functools

import jax
import jax.numpy as jnp
from jax import lax
from jax.experimental import pallas as pl
from jax.experimental.pallas import tpu as pltpu
from jax.sharding import PartitionSpec as P

MESH = pl.DeviceIdType.MESH
F32 = jnp.float32
BF16 = jnp.bfloat16


def split_parts(x):
    hi = x.astype(BF16)
    return hi, (x - hi.astype(F32)).astype(BF16)


def dot(a, b):
    return lax.dot_general(a, b, (((1,), (0,)), ((), ())), preferred_element_type=F32)


def dot_t(a, b):
    return lax.dot_general(a, b, (((1,), (1,)), ((), ())), preferred_element_type=F32)


def iota(shape, axis):
    return lax.broadcasted_iota(jnp.int32, shape, axis)


def kernel(
    lists, helps, depth, cap, crows,
    vec, labels, cent, msrc, mdst, sizes, split_ids, nearby, owner,
    gains, out,
    vhi, vlo, buckets, recv, flag_out, flags, flag_mat, codes, parts, cents, table,
    s_flag, r_flag, s_fgat, r_fgat, s_bkt, r_bkt, s_core, r_core, s_y, r_y, s_rel, r_rel,
    s_part, r_part, s_cent, r_cent,
):
    me = lax.axis_index("lists")
    hp = lax.axis_index("help")
    list_dev, rows, width = vec.shape
    n_rows = list_dev * rows
    moves = mdst.shape[1]
    n_splits, near = nearby.shape
    total_lists = owner.shape[0]
    first = me * list_dev
    core = lax.rem(hp, 2) * -2 + 1 + hp
    far = lax.rem(hp + 2, 4)
    diag = lax.rem(core + 2, 4)

    barrier = pltpu.get_barrier_semaphore()

    def greet(d, c):
        pl.semaphore_signal(
            barrier, inc=1, device_id=(lax.rem(me + d, lists), hp), device_id_type=MESH
        )
        return c

    lax.fori_loop(1, lists, greet, 0)
    for d in range(1, helps):
        pl.semaphore_signal(
            barrier, inc=1, device_id=(me, lax.rem(hp + d, helps)), device_id_type=MESH
        )

    hi, lo = split_parts(vec[...].reshape(n_rows, width))
    vhi[...] = hi
    vlo[...] = lo

    dest = mdst[...]
    slot = jnp.full((1, moves), -1, jnp.int32)
    for x in range(total_lists):
        slot = jnp.where(dest == x, owner[x], slot)
    alive = slot >= 0
    slot_f = slot.astype(F32)
    peer = jnp.where(alive, jnp.floor(slot_f / list_dev), -1.0)
    local = jnp.where(alive, slot_f - peer * list_dev + 1.0, 0.0)
    peer_is = peer == iota((lists, moves), 0).astype(F32)
    peers = jnp.where(peer_is, 1.0, 0.0)
    upper = jnp.where(iota((moves, moves), 0) < iota((moves, moves), 1), 1.0, 0.0).astype(BF16)
    rank = jnp.sum(dot(peers.astype(BF16), upper) * peers, axis=0, keepdims=True)
    at = jnp.where(alive, peer * depth + rank, -1.0).astype(jnp.int32)
    chosen = jnp.where(at == iota((lists * depth, moves), 0), 1.0, 0.0).astype(BF16)
    source = jnp.where(msrc[...] == iota((n_rows, moves), 0), 1.0, 0.0).astype(BF16)
    gather = dot_t(chosen, source).astype(BF16)
    buckets[...] = (dot(gather, hi) + dot(gather, lo)).reshape(lists, depth, width)
    ranked = jnp.where(
        jnp.where(alive, rank, -1.0).astype(jnp.int32) == iota((128, moves), 0), 1.0, 0.0
    ).astype(BF16)
    flag_rows = dot_t(jnp.where(peer_is, local, 0.0).astype(BF16), ranked)
    for p in range(lists):
        flag_out[p] = flag_rows[p : p + 1, :]

    pl.semaphore_wait(barrier, lists - 1 + helps - 1)

    def flag_copy(d):
        return pltpu.make_async_remote_copy(
            src_ref=flag_out.at[lax.rem(me + d, lists)],
            dst_ref=flags.at[hp, me],
            send_sem=s_flag.at[d], recv_sem=r_flag.at[d],
            device_id=(lax.rem(me + d, lists), hp), device_id_type=MESH,
        )

    def bucket_copy(d):
        return pltpu.make_async_remote_copy(
            src_ref=buckets.at[lax.rem(me + d, lists)],
            dst_ref=recv.at[me, hp],
            send_sem=s_bkt.at[d], recv_sem=r_bkt.at[d],
            device_id=(lax.rem(me + d, lists), hp), device_id_type=MESH,
        )

    def cent_copy(d):
        return pltpu.make_async_remote_copy(
            src_ref=cents.at[me], dst_ref=cents.at[me],
            send_sem=s_cent.at[d], recv_sem=r_cent.at[d],
            device_id=(lax.rem(me + d, lists), hp), device_id_type=MESH,
        )

    def help_copy(ref, sends, recvs, d):
        return pltpu.make_async_remote_copy(
            src_ref=ref.at[hp], dst_ref=ref.at[hp],
            send_sem=sends.at[d], recv_sem=recvs.at[d],
            device_id=(me, lax.rem(hp + d, helps)), device_id_type=MESH,
        )

    def piece_copy(d, owner_h, target, sends, recvs):
        piece = recv.at[lax.rem(me + lists - d, lists), owner_h]
        return pltpu.make_async_remote_copy(
            src_ref=piece, dst_ref=piece,
            send_sem=sends.at[d], recv_sem=recvs.at[d],
            device_id=(me, target), device_id_type=MESH,
        )

    def to_core(d):
        return piece_copy(d, hp, core, s_core, r_core)

    def to_far(d):
        return piece_copy(d, hp, far, s_y, r_y)

    def relay(d):
        return piece_copy(d, far, core, s_rel, r_rel)

    def each(lower, upper_, fn):
        def body(d, c):
            fn(d)
            return c

        lax.fori_loop(lower, upper_, body, 0)

    each(1, lists, lambda d: flag_copy(d).start())
    each(1, lists, lambda d: bucket_copy(d).start())
    recv[me, hp] = buckets[me]
    flags[hp, me] = flag_out[me]
    to_core(0).start()
    to_far(0).start()

    lane = iota((crows, n_rows), 1)
    row = iota((crows, n_rows), 0)
    label = jnp.concatenate([labels[k : k + 1, :] for k in range(list_dev)], axis=1)
    limit = jnp.zeros((1, n_rows), jnp.int32)
    lane1 = iota((1, n_rows), 1)
    for k in range(list_dev):
        inside = (lane1 >= k * rows) & (lane1 < (k + 1) * rows)
        limit = jnp.where(inside, sizes[k] + k * rows - hp * rows, limit)
    live_label = jnp.where(lane1 < limit, label, -1)
    half = jnp.zeros((crows, n_rows), F32)
    for k in range(list_dev):
        for a in range(2):
            pick = (row == 2 * k + a) & (lane >= k * rows) & (lane < (k + 1) * rows)
            half = jnp.where(pick & (live_label == a), 1.0, half)
    hb = half.astype(BF16)
    mine = dot(hb, hi) + dot(hb, lo)
    number = jnp.sum(half, axis=1, keepdims=True)
    parts[hp, :, 0:width] = mine
    parts[hp, :, width:] = jnp.broadcast_to(number, (crows, 128))

    for d in range(1, helps):
        help_copy(parts, s_part, r_part, d).start()

    for d in range(1, helps):
        help_copy(parts, s_part, r_part, d).wait_recv()
    summed = parts[0]
    for h in range(1, helps):
        summed = summed + parts[h]
    new_c = summed[:, 0:width] / jnp.maximum(summed[:, width : width + 1], 1.0)
    cents[me] = new_c
    each(1, lists, lambda d: cent_copy(d).start())

    each(1, lists, lambda d: flag_copy(d).wait_recv())
    for d in range(1, helps):
        help_copy(flags, s_fgat, r_fgat, d).start()
    for d in range(1, helps):
        help_copy(flags, s_fgat, r_fgat, d).wait_recv()
    for x in range(lists):
        for h in range(helps):
            flag_mat[x * helps + h : x * helps + h + 1, :] = flags[h, x]
    sources = lists * helps
    flag = flag_mat[...]
    before_lane = jnp.where(iota((128, 128), 0) < iota((128, 128), 1), 1.0, 0.0).astype(BF16)
    before_row = jnp.where(
        iota((sources, sources), 0) > iota((sources, sources), 1), 1.0, 0.0
    ).astype(BF16)
    ones = jnp.ones((128, 128), BF16)
    code = jnp.full((sources, 128), -1.0, F32)
    for k in range(list_dev):
        is_k = flag == float(k + 1)
        one_k = jnp.where(is_k, 1.0, 0.0).astype(BF16)
        place = dot(one_k, before_lane) + dot(before_row, dot(one_k, ones).astype(BF16))
        code = jnp.where(is_k, place + float(k * cap), code)
    spread = jnp.where(iota((sources, 128), 1) < depth, code, 0.0)
    step = depth
    while step < 128:
        spread = spread + pltpu.roll(spread, step, 1)
        step *= 2
    lane_h = iota((sources, 128), 1)
    row_h = lax.rem(iota((sources, 128), 0), helps)
    spread = jnp.where((lane_h >= row_h * depth) & (lane_h < (row_h + 1) * depth), spread, 0.0)
    for x in range(lists):
        codes[x] = jnp.sum(spread[x * helps : (x + 1) * helps, :], axis=0, keepdims=True)

    def ready(d):
        @pl.when(d > 0)
        def _():
            bucket_copy(d).wait_recv()
            to_core(d).start()
            to_far(d).start()

    def pass_on(d):
        to_far(d).wait_recv()
        relay(d).start()

    taken = helps * depth

    def place_piece(d, fresh):
        to_core(d).wait_recv()
        relay(d).wait_recv()
        x = lax.rem(me + lists - d, lists)
        put = codes[x][:, 0:taken].astype(jnp.int32)
        onehot = jnp.where(put == iota((list_dev * cap, taken), 0), 1.0, 0.0).astype(BF16)
        a, b = split_parts(recv[x].reshape(taken, width))
        moved = dot(onehot, a) + dot(onehot, b)
        if fresh:
            out[...] = moved.reshape(list_dev, cap, width)
        else:
            out[...] += moved.reshape(list_dev, cap, width)

    def turn(d):
        ready(d)
        pass_on(d - 1)
        place_piece(d - 2, False)

    ready(1)
    pass_on(0)
    ready(2)
    pass_on(1)
    place_piece(0, True)
    each(3, lists, turn)

    each(1, lists, lambda d: cent_copy(d).wait_recv())
    n_c = lists * crows
    table[0:n_c, :] = cents[...].reshape(n_c, width)
    table[n_c:, :] = jnp.zeros((crows, width), F32)
    for k in range(list_dev):
        table[n_c + k : n_c + k + 1, :] = cent[k : k + 1, :]
    every = table[...]
    c_hi, c_lo = split_parts(every)
    cross = dot_t(c_hi, vhi[...]) + dot_t(c_hi, vlo[...]) + dot_t(c_lo, vhi[...])
    score = jnp.sum(every * every, axis=1, keepdims=True) - 2.0 * cross
    c_row = iota((n_c, rows), 0)
    in_block = lax.rem(c_row, crows)
    slot_of = jnp.where(
        in_block < 2 * list_dev,
        lax.div(c_row, crows) * list_dev + lax.div(in_block, 2),
        -1,
    )
    for k in range(list_dev):
        seen = jnp.zeros((n_c, rows), jnp.int32)
        touched = jnp.int32(0)
        for s in range(n_splits):
            at_slot = owner[split_ids[s]]
            hit = jnp.int32(0)
            for n in range(near):
                hit = jnp.maximum(
                    hit, jnp.where(owner[nearby[s, n]] == first + k, 1, 0).astype(jnp.int32)
                )
            touched = jnp.maximum(touched, hit)
            seen = jnp.maximum(seen, jnp.where(slot_of == at_slot, hit, 0))
        block = score[:, k * rows : (k + 1) * rows]
        best = jnp.min(jnp.where(seen > 0, block[0:n_c], 1e30), axis=0, keepdims=True)
        own = block[n_c + k : n_c + k + 1, :]
        top = jnp.where(touched > 0, sizes[k] - hp * rows, 0)
        ok = iota((1, rows), 1) < top
        gains[k : k + 1, :] = jnp.where(ok, (own - best) * (1.0 / width), 0.0)

    pass_on(lists - 1)
    place_piece(lists - 2, False)
    place_piece(lists - 1, False)

    def drain(d):
        flag_copy(d).wait_send()
        bucket_copy(d).wait_send()
        cent_copy(d).wait_send()

    each(1, lists, drain)

    def drain_pieces(d):
        to_core(d).wait_send()
        to_far(d).wait_send()
        relay(d).wait_send()

    each(0, lists, drain_pieces)
    for d in range(1, helps):
        help_copy(parts, s_part, r_part, d).wait_send()
        help_copy(flags, s_fgat, r_fgat, d).wait_send()


def write_out(gains, arrived, gains_to, arrived_to, sems):
    rows = pltpu.make_async_copy(arrived, arrived_to, sems.at[0])
    few = pltpu.make_async_copy(gains, gains_to, sems.at[1])
    rows.start()
    few.start()
    few.wait()
    rows.wait()


def local(
    vectors, labels, list_sizes, centroids, split_ids, nearby, owner_map, mover_source, mover_dest
):
    list_dev, rows, width = vectors.shape
    lists = lax.axis_size("lists")
    helps = lax.axis_size("help")
    moves = mover_source.shape[0]
    most = max(2, (moves + lists - 1) // lists * 2)
    cap = lists * helps * ((most + list_dev - 1) // list_dev)
    depth = (most + 7) // 8 * 8
    crows = (2 * list_dev + 7) // 8 * 8
    vm = pl.BlockSpec(memory_space=pltpu.VMEM)
    sm = pl.BlockSpec(memory_space=pltpu.SMEM)
    sem = pltpu.SemaphoreType.DMA
    gains, arrived = pl.pallas_call(
        functools.partial(kernel, lists, helps, depth, cap, crows),
        out_shape=(
            pltpu.VMEM((list_dev, rows), F32),
            pltpu.VMEM((list_dev, cap, width), F32),
        ),
        in_specs=[vm] * 5 + [sm] * 4,
        out_specs=(vm, vm),
        scratch_shapes=[
            pltpu.VMEM((list_dev * rows, width), BF16),
            pltpu.VMEM((list_dev * rows, width), BF16),
            pltpu.VMEM((lists, depth, width), F32),
            pltpu.VMEM((lists, helps, depth, width), F32),
            pltpu.VMEM((lists, 1, 128), F32),
            pltpu.VMEM((helps, lists, 1, 128), F32),
            pltpu.VMEM((lists * helps, 128), F32),
            pltpu.VMEM((lists, 1, 128), F32),
            pltpu.VMEM((helps, crows, width + 128), F32),
            pltpu.VMEM((lists, crows, width), F32),
            pltpu.VMEM((lists * crows + crows, width), F32),
            sem((lists,)), sem((lists,)), sem((helps,)), sem((helps,)),
            sem((lists,)), sem((lists,)), sem((lists,)), sem((lists,)),
            sem((lists,)), sem((lists,)), sem((lists,)), sem((lists,)),
            sem((helps,)), sem((helps,)), sem((lists,)), sem((lists,)),
        ],
        compiler_params=pltpu.CompilerParams(
            collective_id=0, has_side_effects=True, vmem_limit_bytes=56 * 1024 * 1024
        ),
    )(
        vectors, labels, centroids, mover_source.reshape(1, moves), mover_dest.reshape(1, moves),
        list_sizes, split_ids, nearby, owner_map,
    )
    hbm = pl.BlockSpec(memory_space=pl.ANY)
    return pl.pallas_call(
        write_out,
        out_shape=(
            jax.ShapeDtypeStruct((list_dev, rows), F32),
            jax.ShapeDtypeStruct((list_dev, cap, width), F32),
        ),
        in_specs=[vm, vm],
        out_specs=(hbm, hbm),
        scratch_shapes=[sem((2,))],
        compiler_params=pltpu.CompilerParams(vmem_limit_bytes=8 * 1024 * 1024),
    )(gains, arrived)


def solution(mesh):
    in_specs = (
        P("lists", "help", None),
        P("lists", "help"),
        P("lists"),
        P("lists", None),
        P(),
        P(),
        P(),
        P(("lists", "help")),
        P(("lists", "help")),
    )
    out_specs = (P("lists", "help"), P("lists", None, None))
    return jax.shard_map(local, mesh=mesh, in_specs=in_specs, out_specs=out_specs, check_vma=False)
```

```python
import functools

import jax
import jax.numpy as jnp
from jax import lax
from jax.experimental import pallas as pl
from jax.experimental.pallas import tpu as pltpu
from jax.sharding import PartitionSpec as P

MESH = pl.DeviceIdType.MESH
F32 = jnp.float32
BF16 = jnp.bfloat16


def split_parts(x):
    hi = x.astype(BF16)
    return hi, (x - hi.astype(F32)).astype(BF16)


def dot(a, b):
    return lax.dot_general(a, b, (((1,), (0,)), ((), ())), preferred_element_type=F32)


def dot_t(a, b):
    return lax.dot_general(a, b, (((1,), (1,)), ((), ())), preferred_element_type=F32)


def iota(shape, axis):
    return lax.broadcasted_iota(jnp.int32, shape, axis)


def kernel(
    lists, helps, depth, cap, crows,
    vec, labels, cent, msrc, mdst, sizes, split_ids, nearby, owner,
    gains, out,
    vhi, vlo, buckets, recv, flag_out, flags, flag_mat, codes, parts, cents, table,
    s_flag, r_flag, s_fgat, r_fgat, s_bkt, r_bkt, s_core, r_core, s_y, r_y, s_rel, r_rel,
    s_part, r_part, s_cent, r_cent,
):
    me = lax.axis_index("lists")
    hp = lax.axis_index("help")
    list_dev, rows, width = vec.shape
    n_rows = list_dev * rows
    moves = mdst.shape[1]
    n_splits, near = nearby.shape
    total_lists = owner.shape[0]
    first = me * list_dev
    core = lax.rem(hp, 2) * -2 + 1 + hp
    far = lax.rem(hp + 2, 4)
    diag = lax.rem(core + 2, 4)

    barrier = pltpu.get_barrier_semaphore()

    def greet(d, c):
        pl.semaphore_signal(
            barrier, inc=1, device_id=(lax.rem(me + d, lists), hp), device_id_type=MESH
        )
        return c

    lax.fori_loop(1, lists, greet, 0)
    for d in range(1, helps):
        pl.semaphore_signal(
            barrier, inc=1, device_id=(me, lax.rem(hp + d, helps)), device_id_type=MESH
        )

    hi, lo = split_parts(vec[...].reshape(n_rows, width))
    vhi[...] = hi
    vlo[...] = lo

    dest = mdst[...]
    slot = jnp.full((1, moves), -1, jnp.int32)
    for x in range(total_lists):
        slot = jnp.where(dest == x, owner[x], slot)
    alive = slot >= 0
    slot_f = slot.astype(F32)
    peer = jnp.where(alive, jnp.floor(slot_f / list_dev), -1.0)
    local = jnp.where(alive, slot_f - peer * list_dev + 1.0, 0.0)
    peer_is = peer == iota((lists, moves), 0).astype(F32)
    peers = jnp.where(peer_is, 1.0, 0.0)
    upper = jnp.where(iota((moves, moves), 0) < iota((moves, moves), 1), 1.0, 0.0).astype(BF16)
    rank = jnp.sum(dot(peers.astype(BF16), upper) * peers, axis=0, keepdims=True)
    at = jnp.where(alive, peer * depth + rank, -1.0).astype(jnp.int32)
    chosen = jnp.where(at == iota((lists * depth, moves), 0), 1.0, 0.0).astype(BF16)
    source = jnp.where(msrc[...] == iota((n_rows, moves), 0), 1.0, 0.0).astype(BF16)
    gather = dot_t(chosen, source).astype(BF16)
    buckets[...] = (dot(gather, hi) + dot(gather, lo)).reshape(lists, depth, width)
    ranked = jnp.where(
        jnp.where(alive, rank, -1.0).astype(jnp.int32) == iota((128, moves), 0), 1.0, 0.0
    ).astype(BF16)
    flag_rows = dot_t(jnp.where(peer_is, local, 0.0).astype(BF16), ranked)
    for p in range(lists):
        flag_out[p] = flag_rows[p : p + 1, :]

    pl.semaphore_wait(barrier, lists - 1 + helps - 1)

    def hop(k):
        k = jnp.int32(k)
        j = k - 1
        turn_ = 1 - 2 * lax.rem(j + 2, 2)
        away = lists // 2 + turn_ * lax.div(j + 1, 2)
        return away * jnp.minimum(k, 1)

    def flag_copy(d):
        return pltpu.make_async_remote_copy(
            src_ref=flag_out.at[lax.rem(me + d, lists)],
            dst_ref=flags.at[hp, me],
            send_sem=s_flag.at[d], recv_sem=r_flag.at[d],
            device_id=(lax.rem(me + d, lists), hp), device_id_type=MESH,
        )

    def bucket_copy(d):
        return pltpu.make_async_remote_copy(
            src_ref=buckets.at[lax.rem(me + hop(d), lists)],
            dst_ref=recv.at[me, hp],
            send_sem=s_bkt.at[d], recv_sem=r_bkt.at[d],
            device_id=(lax.rem(me + hop(d), lists), hp), device_id_type=MESH,
        )

    def cent_copy(d):
        return pltpu.make_async_remote_copy(
            src_ref=cents.at[me], dst_ref=cents.at[me],
            send_sem=s_cent.at[d], recv_sem=r_cent.at[d],
            device_id=(lax.rem(me + d, lists), hp), device_id_type=MESH,
        )

    def help_copy(ref, sends, recvs, d):
        return pltpu.make_async_remote_copy(
            src_ref=ref.at[hp], dst_ref=ref.at[hp],
            send_sem=sends.at[d], recv_sem=recvs.at[d],
            device_id=(me, lax.rem(hp + d, helps)), device_id_type=MESH,
        )

    def piece_copy(d, owner_h, target, sends, recvs):
        piece = recv.at[lax.rem(me + lists - hop(d), lists), owner_h]
        return pltpu.make_async_remote_copy(
            src_ref=piece, dst_ref=piece,
            send_sem=sends.at[d], recv_sem=recvs.at[d],
            device_id=(me, target), device_id_type=MESH,
        )

    def to_core(d):
        return piece_copy(d, hp, core, s_core, r_core)

    def to_far(d):
        return piece_copy(d, hp, far, s_y, r_y)

    def relay(d):
        return piece_copy(d, far, core, s_rel, r_rel)

    def each(lower, upper_, fn):
        def body(d, c):
            fn(d)
            return c

        lax.fori_loop(lower, upper_, body, 0)

    each(1, lists, lambda d: flag_copy(d).start())
    each(1, lists, lambda d: bucket_copy(d).start())
    recv[me, hp] = buckets[me]
    flags[hp, me] = flag_out[me]
    to_core(0).start()
    to_far(0).start()

    lane = iota((crows, n_rows), 1)
    row = iota((crows, n_rows), 0)
    label = jnp.concatenate([labels[k : k + 1, :] for k in range(list_dev)], axis=1)
    limit = jnp.zeros((1, n_rows), jnp.int32)
    lane1 = iota((1, n_rows), 1)
    for k in range(list_dev):
        inside = (lane1 >= k * rows) & (lane1 < (k + 1) * rows)
        limit = jnp.where(inside, sizes[k] + k * rows - hp * rows, limit)
    live_label = jnp.where(lane1 < limit, label, -1)
    half = jnp.zeros((crows, n_rows), F32)
    for k in range(list_dev):
        for a in range(2):
            pick = (row == 2 * k + a) & (lane >= k * rows) & (lane < (k + 1) * rows)
            half = jnp.where(pick & (live_label == a), 1.0, half)
    hb = half.astype(BF16)
    mine = dot(hb, hi) + dot(hb, lo)
    number = jnp.sum(half, axis=1, keepdims=True)
    parts[hp, :, 0:width] = mine
    parts[hp, :, width:] = jnp.broadcast_to(number, (crows, 128))

    for d in range(1, helps):
        help_copy(parts, s_part, r_part, d).start()

    for d in range(1, helps):
        help_copy(parts, s_part, r_part, d).wait_recv()
    summed = parts[0]
    for h in range(1, helps):
        summed = summed + parts[h]
    new_c = summed[:, 0:width] / jnp.maximum(summed[:, width : width + 1], 1.0)
    cents[me] = new_c
    each(1, lists, lambda d: cent_copy(d).start())

    each(1, lists, lambda d: flag_copy(d).wait_recv())
    for d in range(1, helps):
        help_copy(flags, s_fgat, r_fgat, d).start()
    for d in range(1, helps):
        help_copy(flags, s_fgat, r_fgat, d).wait_recv()
    for x in range(lists):
        for h in range(helps):
            flag_mat[x * helps + h : x * helps + h + 1, :] = flags[h, x]
    sources = lists * helps
    flag = flag_mat[...]
    before_lane = jnp.where(iota((128, 128), 0) < iota((128, 128), 1), 1.0, 0.0).astype(BF16)
    before_row = jnp.where(
        iota((sources, sources), 0) > iota((sources, sources), 1), 1.0, 0.0
    ).astype(BF16)
    ones = jnp.ones((128, 128), BF16)
    code = jnp.full((sources, 128), -1.0, F32)
    for k in range(list_dev):
        is_k = flag == float(k + 1)
        one_k = jnp.where(is_k, 1.0, 0.0).astype(BF16)
        place = dot(one_k, before_lane) + dot(before_row, dot(one_k, ones).astype(BF16))
        code = jnp.where(is_k, place + float(k * cap), code)
    spread = jnp.where(iota((sources, 128), 1) < depth, code, 0.0)
    step = depth
    while step < 128:
        spread = spread + pltpu.roll(spread, step, 1)
        step *= 2
    lane_h = iota((sources, 128), 1)
    row_h = lax.rem(iota((sources, 128), 0), helps)
    spread = jnp.where((lane_h >= row_h * depth) & (lane_h < (row_h + 1) * depth), spread, 0.0)
    for x in range(lists):
        codes[x] = jnp.sum(spread[x * helps : (x + 1) * helps, :], axis=0, keepdims=True)

    def ready(d):
        @pl.when(d > 0)
        def _():
            bucket_copy(d).wait_recv()
            to_core(d).start()
            to_far(d).start()

    def pass_on(d):
        to_far(d).wait_recv()
        relay(d).start()

    taken = helps * depth

    def place_piece(d, fresh):
        to_core(d).wait_recv()
        relay(d).wait_recv()
        x = lax.rem(me + lists - hop(d), lists)
        put = codes[x][:, 0:taken].astype(jnp.int32)
        onehot = jnp.where(put == iota((list_dev * cap, taken), 0), 1.0, 0.0).astype(BF16)
        a, b = split_parts(recv[x].reshape(taken, width))
        moved = dot(onehot, a) + dot(onehot, b)
        if fresh:
            out[...] = moved.reshape(list_dev, cap, width)
        else:
            out[...] += moved.reshape(list_dev, cap, width)

    def turn(d):
        ready(d)
        pass_on(d - 1)
        place_piece(d - 2, False)

    ready(1)
    pass_on(0)
    ready(2)
    pass_on(1)
    place_piece(0, True)
    each(3, lists, turn)

    each(1, lists, lambda d: cent_copy(d).wait_recv())
    n_c = lists * crows
    table[0:n_c, :] = cents[...].reshape(n_c, width)
    table[n_c:, :] = jnp.zeros((crows, width), F32)
    for k in range(list_dev):
        table[n_c + k : n_c + k + 1, :] = cent[k : k + 1, :]
    every = table[...]
    c_hi, c_lo = split_parts(every)
    cross = dot_t(c_hi, vhi[...]) + dot_t(c_hi, vlo[...]) + dot_t(c_lo, vhi[...])
    score = jnp.sum(every * every, axis=1, keepdims=True) - 2.0 * cross
    c_row = iota((n_c, rows), 0)
    in_block = lax.rem(c_row, crows)
    slot_of = jnp.where(
        in_block < 2 * list_dev,
        lax.div(c_row, crows) * list_dev + lax.div(in_block, 2),
        -1,
    )
    for k in range(list_dev):
        seen = jnp.zeros((n_c, rows), jnp.int32)
        touched = jnp.int32(0)
        for s in range(n_splits):
            at_slot = owner[split_ids[s]]
            hit = jnp.int32(0)
            for n in range(near):
                hit = jnp.maximum(
                    hit, jnp.where(owner[nearby[s, n]] == first + k, 1, 0).astype(jnp.int32)
                )
            touched = jnp.maximum(touched, hit)
            seen = jnp.maximum(seen, jnp.where(slot_of == at_slot, hit, 0))
        block = score[:, k * rows : (k + 1) * rows]
        best = jnp.min(jnp.where(seen > 0, block[0:n_c], 1e30), axis=0, keepdims=True)
        own = block[n_c + k : n_c + k + 1, :]
        top = jnp.where(touched > 0, sizes[k] - hp * rows, 0)
        ok = iota((1, rows), 1) < top
        gains[k : k + 1, :] = jnp.where(ok, (own - best) * (1.0 / width), 0.0)

    pass_on(lists - 1)
    place_piece(lists - 2, False)
    place_piece(lists - 1, False)

    def drain(d):
        flag_copy(d).wait_send()
        bucket_copy(d).wait_send()
        cent_copy(d).wait_send()

    each(1, lists, drain)

    def drain_pieces(d):
        to_core(d).wait_send()
        to_far(d).wait_send()
        relay(d).wait_send()

    each(0, lists, drain_pieces)
    for d in range(1, helps):
        help_copy(parts, s_part, r_part, d).wait_send()
        help_copy(flags, s_fgat, r_fgat, d).wait_send()


def write_out(gains, arrived, gains_to, arrived_to, sems):
    rows = pltpu.make_async_copy(arrived, arrived_to, sems.at[0])
    few = pltpu.make_async_copy(gains, gains_to, sems.at[1])
    rows.start()
    few.start()
    few.wait()
    rows.wait()


def local(
    vectors, labels, list_sizes, centroids, split_ids, nearby, owner_map, mover_source, mover_dest
):
    list_dev, rows, width = vectors.shape
    lists = lax.axis_size("lists")
    helps = lax.axis_size("help")
    moves = mover_source.shape[0]
    most = max(2, (moves + lists - 1) // lists * 2)
    cap = lists * helps * ((most + list_dev - 1) // list_dev)
    depth = (most + 7) // 8 * 8
    crows = (2 * list_dev + 7) // 8 * 8
    vm = pl.BlockSpec(memory_space=pltpu.VMEM)
    sm = pl.BlockSpec(memory_space=pltpu.SMEM)
    sem = pltpu.SemaphoreType.DMA
    gains, arrived = pl.pallas_call(
        functools.partial(kernel, lists, helps, depth, cap, crows),
        out_shape=(
            pltpu.VMEM((list_dev, rows), F32),
            pltpu.VMEM((list_dev, cap, width), F32),
        ),
        in_specs=[vm] * 5 + [sm] * 4,
        out_specs=(vm, vm),
        scratch_shapes=[
            pltpu.VMEM((list_dev * rows, width), BF16),
            pltpu.VMEM((list_dev * rows, width), BF16),
            pltpu.VMEM((lists, depth, width), F32),
            pltpu.VMEM((lists, helps, depth, width), F32),
            pltpu.VMEM((lists, 1, 128), F32),
            pltpu.VMEM((helps, lists, 1, 128), F32),
            pltpu.VMEM((lists * helps, 128), F32),
            pltpu.VMEM((lists, 1, 128), F32),
            pltpu.VMEM((helps, crows, width + 128), F32),
            pltpu.VMEM((lists, crows, width), F32),
            pltpu.VMEM((lists * crows + crows, width), F32),
            sem((lists,)), sem((lists,)), sem((helps,)), sem((helps,)),
            sem((lists,)), sem((lists,)), sem((lists,)), sem((lists,)),
            sem((lists,)), sem((lists,)), sem((lists,)), sem((lists,)),
            sem((helps,)), sem((helps,)), sem((lists,)), sem((lists,)),
        ],
        compiler_params=pltpu.CompilerParams(
            collective_id=0, has_side_effects=True, vmem_limit_bytes=56 * 1024 * 1024
        ),
    )(
        vectors, labels, centroids, mover_source.reshape(1, moves), mover_dest.reshape(1, moves),
        list_sizes, split_ids, nearby, owner_map,
    )
    hbm = pl.BlockSpec(memory_space=pl.ANY)
    return pl.pallas_call(
        write_out,
        out_shape=(
            jax.ShapeDtypeStruct((list_dev, rows), F32),
            jax.ShapeDtypeStruct((list_dev, cap, width), F32),
        ),
        in_specs=[vm, vm],
        out_specs=(hbm, hbm),
        scratch_shapes=[sem((2,))],
        compiler_params=pltpu.CompilerParams(vmem_limit_bytes=8 * 1024 * 1024),
    )(gains, arrived)


def solution(mesh):
    in_specs = (
        P("lists", "help", None),
        P("lists", "help"),
        P("lists"),
        P("lists", None),
        P(),
        P(),
        P(),
        P(("lists", "help")),
        P(("lists", "help")),
    )
    out_specs = (P("lists", "help"), P("lists", None, None))
    return jax.shard_map(local, mesh=mesh, in_specs=in_specs, out_specs=out_specs, check_vma=False)
```

```python
import functools

import jax
import jax.numpy as jnp
from jax import lax
from jax.experimental import pallas as pl
from jax.experimental.pallas import tpu as pltpu
from jax.sharding import PartitionSpec as P

MESH = pl.DeviceIdType.MESH
F32 = jnp.float32
BF16 = jnp.bfloat16


def split_parts(x):
    hi = x.astype(BF16)
    return hi, (x - hi.astype(F32)).astype(BF16)


def dot(a, b):
    return lax.dot_general(a, b, (((1,), (0,)), ((), ())), preferred_element_type=F32)


def dot_t(a, b):
    return lax.dot_general(a, b, (((1,), (1,)), ((), ())), preferred_element_type=F32)


def iota(shape, axis):
    return lax.broadcasted_iota(jnp.int32, shape, axis)


def kernel(
    lists, helps, depth, cap, crows,
    vec, labels, cent, msrc, mdst, sizes, split_ids, nearby, owner,
    gains, out,
    vhi, vlo, buckets, recv, flag_out, flags, flag_mat, codes, parts, cents, table,
    s_flag, r_flag, s_fgat, r_fgat, s_bkt, r_bkt, s_core, r_core, s_y, r_y, s_rel, r_rel,
    s_part, r_part, s_cent, r_cent,
):
    me = lax.axis_index("lists")
    hp = lax.axis_index("help")
    list_dev, rows, width = vec.shape
    n_rows = list_dev * rows
    moves = mdst.shape[1]
    n_splits, near = nearby.shape
    total_lists = owner.shape[0]
    first = me * list_dev
    core = lax.rem(hp, 2) * -2 + 1 + hp
    far = lax.rem(hp + 2, 4)
    diag = lax.rem(core + 2, 4)

    barrier = pltpu.get_barrier_semaphore()

    def greet(d, c):
        pl.semaphore_signal(
            barrier, inc=1, device_id=(lax.rem(me + d, lists), hp), device_id_type=MESH
        )
        return c

    lax.fori_loop(1, lists, greet, 0)
    for d in range(1, helps):
        pl.semaphore_signal(
            barrier, inc=1, device_id=(me, lax.rem(hp + d, helps)), device_id_type=MESH
        )

    hi, lo = split_parts(vec[...].reshape(n_rows, width))
    vhi[...] = hi
    vlo[...] = lo

    dest = mdst[...]
    slot = jnp.full((1, moves), -1, jnp.int32)
    for x in range(total_lists):
        slot = jnp.where(dest == x, owner[x], slot)
    alive = slot >= 0
    slot_f = slot.astype(F32)
    peer = jnp.where(alive, jnp.floor(slot_f / list_dev), -1.0)
    local = jnp.where(alive, slot_f - peer * list_dev + 1.0, 0.0)
    peer_is = peer == iota((lists, moves), 0).astype(F32)
    peers = jnp.where(peer_is, 1.0, 0.0)
    upper = jnp.where(iota((moves, moves), 0) < iota((moves, moves), 1), 1.0, 0.0).astype(BF16)
    rank = jnp.sum(dot(peers.astype(BF16), upper) * peers, axis=0, keepdims=True)
    at = jnp.where(alive, peer * depth + rank, -1.0).astype(jnp.int32)
    chosen = jnp.where(at == iota((lists * depth, moves), 0), 1.0, 0.0).astype(BF16)
    source = jnp.where(msrc[...] == iota((n_rows, moves), 0), 1.0, 0.0).astype(BF16)
    gather = dot_t(chosen, source).astype(BF16)
    buckets[...] = (dot(gather, hi) + dot(gather, lo)).reshape(lists, depth, width)
    ranked = jnp.where(
        jnp.where(alive, rank, -1.0).astype(jnp.int32) == iota((128, moves), 0), 1.0, 0.0
    ).astype(BF16)
    flag_rows = dot_t(jnp.where(peer_is, local, 0.0).astype(BF16), ranked)
    for p in range(lists):
        flag_out[p] = flag_rows[p : p + 1, :]

    pl.semaphore_wait(barrier, lists - 1 + helps - 1)

    def hop(k):
        k = jnp.int32(k)
        j = k - 1
        turn_ = 1 - 2 * lax.rem(j + 2, 2)
        away = lists // 2 + turn_ * lax.div(j + 1, 2)
        return away * jnp.minimum(k, 1)

    def flag_copy(d):
        return pltpu.make_async_remote_copy(
            src_ref=flag_out.at[lax.rem(me + d, lists)],
            dst_ref=flags.at[hp, me],
            send_sem=s_flag.at[d], recv_sem=r_flag.at[d],
            device_id=(lax.rem(me + d, lists), hp), device_id_type=MESH,
        )

    def bucket_copy(d):
        return pltpu.make_async_remote_copy(
            src_ref=buckets.at[lax.rem(me + hop(d), lists)],
            dst_ref=recv.at[me, hp],
            send_sem=s_bkt.at[d], recv_sem=r_bkt.at[d],
            device_id=(lax.rem(me + hop(d), lists), hp), device_id_type=MESH,
        )

    def cent_copy(d):
        return pltpu.make_async_remote_copy(
            src_ref=cents.at[me], dst_ref=cents.at[me],
            send_sem=s_cent.at[d], recv_sem=r_cent.at[d],
            device_id=(lax.rem(me + d, lists), hp), device_id_type=MESH,
        )

    def help_copy(ref, sends, recvs, d):
        return pltpu.make_async_remote_copy(
            src_ref=ref.at[hp], dst_ref=ref.at[hp],
            send_sem=sends.at[d], recv_sem=recvs.at[d],
            device_id=(me, lax.rem(hp + d, helps)), device_id_type=MESH,
        )

    def piece_copy(d, owner_h, target, sends, recvs):
        piece = recv.at[lax.rem(me + lists - hop(d), lists), owner_h]
        return pltpu.make_async_remote_copy(
            src_ref=piece, dst_ref=piece,
            send_sem=sends.at[d], recv_sem=recvs.at[d],
            device_id=(me, target), device_id_type=MESH,
        )

    def to_core(d):
        return piece_copy(d, hp, core, s_core, r_core)

    def to_far(d):
        return piece_copy(d, hp, far, s_y, r_y)

    def relay(d):
        return piece_copy(d, far, core, s_rel, r_rel)

    def each(lower, upper_, fn):
        def body(d, c):
            fn(d)
            return c

        lax.fori_loop(lower, upper_, body, 0)

    each(1, lists, lambda d: flag_copy(d).start())
    each(1, lists, lambda d: bucket_copy(d).start())
    recv[me, hp] = buckets[me]
    flags[hp, me] = flag_out[me]
    to_core(0).start()
    to_far(0).start()

    lane = iota((crows, n_rows), 1)
    row = iota((crows, n_rows), 0)
    label = jnp.concatenate([labels[k : k + 1, :] for k in range(list_dev)], axis=1)
    limit = jnp.zeros((1, n_rows), jnp.int32)
    lane1 = iota((1, n_rows), 1)
    for k in range(list_dev):
        inside = (lane1 >= k * rows) & (lane1 < (k + 1) * rows)
        limit = jnp.where(inside, sizes[k] + k * rows - hp * rows, limit)
    live_label = jnp.where(lane1 < limit, label, -1)
    half = jnp.zeros((crows, n_rows), F32)
    for k in range(list_dev):
        for a in range(2):
            pick = (row == 2 * k + a) & (lane >= k * rows) & (lane < (k + 1) * rows)
            half = jnp.where(pick & (live_label == a), 1.0, half)
    hb = half.astype(BF16)
    mine = dot(hb, hi) + dot(hb, lo)
    number = jnp.sum(half, axis=1, keepdims=True)
    parts[hp, :, 0:width] = mine
    parts[hp, :, width:] = jnp.broadcast_to(number, (crows, 128))

    for d in range(1, helps):
        help_copy(parts, s_part, r_part, d).start()

    for d in range(1, helps):
        help_copy(parts, s_part, r_part, d).wait_recv()
    summed = parts[0]
    for h in range(1, helps):
        summed = summed + parts[h]
    new_c = summed[:, 0:width] / jnp.maximum(summed[:, width : width + 1], 1.0)
    cents[me] = new_c
    each(1, lists, lambda d: cent_copy(d).start())

    each(1, lists, lambda d: flag_copy(d).wait_recv())
    for d in range(1, helps):
        help_copy(flags, s_fgat, r_fgat, d).start()
    for d in range(1, helps):
        help_copy(flags, s_fgat, r_fgat, d).wait_recv()
    for x in range(lists):
        for h in range(helps):
            flag_mat[x * helps + h : x * helps + h + 1, :] = flags[h, x]
    sources = lists * helps
    flag = flag_mat[...]
    before_lane = jnp.where(iota((128, 128), 0) < iota((128, 128), 1), 1.0, 0.0).astype(BF16)
    before_row = jnp.where(
        iota((sources, sources), 0) > iota((sources, sources), 1), 1.0, 0.0
    ).astype(BF16)
    ones = jnp.ones((128, 128), BF16)
    code = jnp.full((sources, 128), -1.0, F32)
    for k in range(list_dev):
        is_k = flag == float(k + 1)
        one_k = jnp.where(is_k, 1.0, 0.0).astype(BF16)
        place = dot(one_k, before_lane) + dot(before_row, dot(one_k, ones).astype(BF16))
        code = jnp.where(is_k, place + float(k * cap), code)
    spread = jnp.where(iota((sources, 128), 1) < depth, code, 0.0)
    step = depth
    while step < 128:
        spread = spread + pltpu.roll(spread, step, 1)
        step *= 2
    lane_h = iota((sources, 128), 1)
    row_h = lax.rem(iota((sources, 128), 0), helps)
    spread = jnp.where((lane_h >= row_h * depth) & (lane_h < (row_h + 1) * depth), spread, 0.0)
    for x in range(lists):
        codes[x] = jnp.sum(spread[x * helps : (x + 1) * helps, :], axis=0, keepdims=True)

    def ready(d):
        @pl.when(d > 0)
        def _():
            bucket_copy(d).wait_recv()
            to_core(d).start()
            to_far(d).start()

    def pass_on(d):
        to_far(d).wait_recv()
        relay(d).start()

    taken = helps * depth

    def place_piece(d, fresh):
        to_core(d).wait_recv()
        relay(d).wait_recv()
        x = lax.rem(me + lists - hop(d), lists)
        put = codes[x][:, 0:taken].astype(jnp.int32)
        onehot = jnp.where(put == iota((list_dev * cap, taken), 0), 1.0, 0.0).astype(BF16)
        a, b = split_parts(recv[x].reshape(taken, width))
        if taken % 128 == 0:
            moved = dot(
                jnp.concatenate([onehot, onehot], axis=1), jnp.concatenate([a, b], axis=0)
            )
        else:
            moved = dot(onehot, a) + dot(onehot, b)
        if fresh:
            out[...] = moved.reshape(list_dev, cap, width)
        else:
            out[...] += moved.reshape(list_dev, cap, width)

    def turn(d):
        ready(d)
        pass_on(d - 1)
        place_piece(d - 2, False)

    ready(1)
    pass_on(0)
    ready(2)
    pass_on(1)
    place_piece(0, True)
    each(3, lists, turn)

    each(1, lists, lambda d: cent_copy(d).wait_recv())
    n_c = lists * crows
    table[0:n_c, :] = cents[...].reshape(n_c, width)
    table[n_c:, :] = jnp.zeros((crows, width), F32)
    for k in range(list_dev):
        table[n_c + k : n_c + k + 1, :] = cent[k : k + 1, :]
    every = table[...]
    c_hi, c_lo = split_parts(every)
    cross = dot_t(c_hi, vhi[...]) + dot_t(c_hi, vlo[...]) + dot_t(c_lo, vhi[...])
    score = jnp.sum(every * every, axis=1, keepdims=True) - 2.0 * cross
    c_row = iota((n_c, rows), 0)
    in_block = lax.rem(c_row, crows)
    slot_of = jnp.where(
        in_block < 2 * list_dev,
        lax.div(c_row, crows) * list_dev + lax.div(in_block, 2),
        -1,
    )
    for k in range(list_dev):
        seen = jnp.zeros((n_c, rows), jnp.int32)
        touched = jnp.int32(0)
        for s in range(n_splits):
            at_slot = owner[split_ids[s]]
            hit = jnp.int32(0)
            for n in range(near):
                hit = jnp.maximum(
                    hit, jnp.where(owner[nearby[s, n]] == first + k, 1, 0).astype(jnp.int32)
                )
            touched = jnp.maximum(touched, hit)
            seen = jnp.maximum(seen, jnp.where(slot_of == at_slot, hit, 0))
        block = score[:, k * rows : (k + 1) * rows]
        best = jnp.min(jnp.where(seen > 0, block[0:n_c], 1e30), axis=0, keepdims=True)
        own = block[n_c + k : n_c + k + 1, :]
        top = jnp.where(touched > 0, sizes[k] - hp * rows, 0)
        ok = iota((1, rows), 1) < top
        gains[k : k + 1, :] = jnp.where(ok, (own - best) * (1.0 / width), 0.0)

    pass_on(lists - 1)
    place_piece(lists - 2, False)
    place_piece(lists - 1, False)

    def drain(d):
        flag_copy(d).wait_send()
        bucket_copy(d).wait_send()
        cent_copy(d).wait_send()

    each(1, lists, drain)

    def drain_pieces(d):
        to_core(d).wait_send()
        to_far(d).wait_send()
        relay(d).wait_send()

    each(0, lists, drain_pieces)
    for d in range(1, helps):
        help_copy(parts, s_part, r_part, d).wait_send()
        help_copy(flags, s_fgat, r_fgat, d).wait_send()


def write_out(gains, arrived, gains_to, arrived_to, sems):
    rows = pltpu.make_async_copy(arrived, arrived_to, sems.at[0])
    few = pltpu.make_async_copy(gains, gains_to, sems.at[1])
    rows.start()
    few.start()
    few.wait()
    rows.wait()


def local(
    vectors, labels, list_sizes, centroids, split_ids, nearby, owner_map, mover_source, mover_dest
):
    list_dev, rows, width = vectors.shape
    lists = lax.axis_size("lists")
    helps = lax.axis_size("help")
    moves = mover_source.shape[0]
    most = max(2, (moves + lists - 1) // lists * 2)
    cap = lists * helps * ((most + list_dev - 1) // list_dev)
    depth = (most + 7) // 8 * 8
    crows = (2 * list_dev + 7) // 8 * 8
    vm = pl.BlockSpec(memory_space=pltpu.VMEM)
    sm = pl.BlockSpec(memory_space=pltpu.SMEM)
    sem = pltpu.SemaphoreType.DMA
    gains, arrived = pl.pallas_call(
        functools.partial(kernel, lists, helps, depth, cap, crows),
        out_shape=(
            pltpu.VMEM((list_dev, rows), F32),
            pltpu.VMEM((list_dev, cap, width), F32),
        ),
        in_specs=[vm] * 5 + [sm] * 4,
        out_specs=(vm, vm),
        scratch_shapes=[
            pltpu.VMEM((list_dev * rows, width), BF16),
            pltpu.VMEM((list_dev * rows, width), BF16),
            pltpu.VMEM((lists, depth, width), F32),
            pltpu.VMEM((lists, helps, depth, width), F32),
            pltpu.VMEM((lists, 1, 128), F32),
            pltpu.VMEM((helps, lists, 1, 128), F32),
            pltpu.VMEM((lists * helps, 128), F32),
            pltpu.VMEM((lists, 1, 128), F32),
            pltpu.VMEM((helps, crows, width + 128), F32),
            pltpu.VMEM((lists, crows, width), F32),
            pltpu.VMEM((lists * crows + crows, width), F32),
            sem((lists,)), sem((lists,)), sem((helps,)), sem((helps,)),
            sem((lists,)), sem((lists,)), sem((lists,)), sem((lists,)),
            sem((lists,)), sem((lists,)), sem((lists,)), sem((lists,)),
            sem((helps,)), sem((helps,)), sem((lists,)), sem((lists,)),
        ],
        compiler_params=pltpu.CompilerParams(
            collective_id=0, has_side_effects=True, vmem_limit_bytes=56 * 1024 * 1024
        ),
    )(
        vectors, labels, centroids, mover_source.reshape(1, moves), mover_dest.reshape(1, moves),
        list_sizes, split_ids, nearby, owner_map,
    )
    hbm = pl.BlockSpec(memory_space=pl.ANY)
    return pl.pallas_call(
        write_out,
        out_shape=(
            jax.ShapeDtypeStruct((list_dev, rows), F32),
            jax.ShapeDtypeStruct((list_dev, cap, width), F32),
        ),
        in_specs=[vm, vm],
        out_specs=(hbm, hbm),
        scratch_shapes=[sem((2,))],
        compiler_params=pltpu.CompilerParams(vmem_limit_bytes=8 * 1024 * 1024),
    )(gains, arrived)


def solution(mesh):
    in_specs = (
        P("lists", "help", None),
        P("lists", "help"),
        P("lists"),
        P("lists", None),
        P(),
        P(),
        P(),
        P(("lists", "help")),
        P(("lists", "help")),
    )
    out_specs = (P("lists", "help"), P("lists", None, None))
    return jax.shard_map(local, mesh=mesh, in_specs=in_specs, out_specs=out_specs, check_vma=False)
```

```python
import functools

import jax
import jax.numpy as jnp
from jax import lax
from jax.experimental import pallas as pl
from jax.experimental.pallas import tpu as pltpu
from jax.sharding import PartitionSpec as P

MESH = pl.DeviceIdType.MESH
F32 = jnp.float32
BF16 = jnp.bfloat16


def split_parts(x):
    hi = x.astype(BF16)
    return hi, (x - hi.astype(F32)).astype(BF16)


def dot(a, b):
    return lax.dot_general(a, b, (((1,), (0,)), ((), ())), preferred_element_type=F32)


def dot_t(a, b):
    return lax.dot_general(a, b, (((1,), (1,)), ((), ())), preferred_element_type=F32)


def iota(shape, axis):
    return lax.broadcasted_iota(jnp.int32, shape, axis)


def kernel(
    lists, helps, depth, cap, crows,
    vec, labels, cent, msrc, mdst, sizes, split_ids, nearby, owner,
    gains, out,
    vhi, vlo, buckets, recv, flag_out, flags, flag_mat, codes, parts, cents, table,
    s_flag, r_flag, s_fgat, r_fgat, s_bkt, r_bkt, s_core, r_core, s_y, r_y, s_rel, r_rel,
    s_part, r_part, s_cent, r_cent,
):
    me = lax.axis_index("lists")
    hp = lax.axis_index("help")
    list_dev, rows, width = vec.shape
    n_rows = list_dev * rows
    moves = mdst.shape[1]
    n_splits, near = nearby.shape
    total_lists = owner.shape[0]
    first = me * list_dev
    core = lax.rem(hp, 2) * -2 + 1 + hp
    far = lax.rem(hp + 2, 4)
    diag = lax.rem(core + 2, 4)

    barrier = pltpu.get_barrier_semaphore()

    def greet(d, c):
        pl.semaphore_signal(
            barrier, inc=1, device_id=(lax.rem(me + d, lists), hp), device_id_type=MESH
        )
        return c

    lax.fori_loop(1, lists, greet, 0)
    for d in range(1, helps):
        pl.semaphore_signal(
            barrier, inc=1, device_id=(me, lax.rem(hp + d, helps)), device_id_type=MESH
        )

    hi, lo = split_parts(vec[...].reshape(n_rows, width))
    vhi[...] = hi
    vlo[...] = lo

    dest = mdst[...]
    slot = jnp.full((1, moves), -1, jnp.int32)
    for x in range(total_lists):
        slot = jnp.where(dest == x, owner[x], slot)
    alive = slot >= 0
    slot_f = slot.astype(F32)
    peer = jnp.where(alive, jnp.floor(slot_f / list_dev), -1.0)
    local = jnp.where(alive, slot_f - peer * list_dev + 1.0, 0.0)
    peer_is = peer == iota((lists, moves), 0).astype(F32)
    peers = jnp.where(peer_is, 1.0, 0.0)
    upper = jnp.where(iota((moves, moves), 0) < iota((moves, moves), 1), 1.0, 0.0).astype(BF16)
    rank = jnp.sum(dot(peers.astype(BF16), upper) * peers, axis=0, keepdims=True)
    at = jnp.where(alive, peer * depth + rank, -1.0).astype(jnp.int32)
    chosen = jnp.where(at == iota((lists * depth, moves), 0), 1.0, 0.0).astype(BF16)
    source = jnp.where(msrc[...] == iota((n_rows, moves), 0), 1.0, 0.0).astype(BF16)
    gather = dot_t(chosen, source).astype(BF16)
    buckets[...] = (dot(gather, hi) + dot(gather, lo)).reshape(lists, depth, width)
    ranked = jnp.where(
        jnp.where(alive, rank, -1.0).astype(jnp.int32) == iota((128, moves), 0), 1.0, 0.0
    ).astype(BF16)
    flag_rows = dot_t(jnp.where(peer_is, local, 0.0).astype(BF16), ranked)
    for p in range(lists):
        flag_out[p] = flag_rows[p : p + 1, :]

    pl.semaphore_wait(barrier, lists - 1 + helps - 1)

    def hop(k):
        k = jnp.int32(k)
        j = k - 1
        turn_ = 1 - 2 * lax.rem(j + 2, 2)
        away = lists // 2 + turn_ * lax.div(j + 1, 2)
        return away * jnp.minimum(k, 1)

    def flag_copy(d):
        return pltpu.make_async_remote_copy(
            src_ref=flag_out.at[lax.rem(me + d, lists)],
            dst_ref=flags.at[hp, me],
            send_sem=s_flag.at[d], recv_sem=r_flag.at[d],
            device_id=(lax.rem(me + d, lists), hp), device_id_type=MESH,
        )

    def bucket_copy(d):
        return pltpu.make_async_remote_copy(
            src_ref=buckets.at[lax.rem(me + hop(d), lists)],
            dst_ref=recv.at[me, hp],
            send_sem=s_bkt.at[d], recv_sem=r_bkt.at[d],
            device_id=(lax.rem(me + hop(d), lists), hp), device_id_type=MESH,
        )

    def cent_copy(d):
        return pltpu.make_async_remote_copy(
            src_ref=cents.at[me], dst_ref=cents.at[me],
            send_sem=s_cent.at[d], recv_sem=r_cent.at[d],
            device_id=(lax.rem(me + d, lists), hp), device_id_type=MESH,
        )

    def help_copy(ref, sends, recvs, d):
        return pltpu.make_async_remote_copy(
            src_ref=ref.at[hp], dst_ref=ref.at[hp],
            send_sem=sends.at[d], recv_sem=recvs.at[d],
            device_id=(me, lax.rem(hp + d, helps)), device_id_type=MESH,
        )

    def piece_copy(d, owner_h, target, sends, recvs):
        piece = recv.at[lax.rem(me + lists - hop(d), lists), owner_h]
        return pltpu.make_async_remote_copy(
            src_ref=piece, dst_ref=piece,
            send_sem=sends.at[d], recv_sem=recvs.at[d],
            device_id=(me, target), device_id_type=MESH,
        )

    def to_core(d):
        return piece_copy(d, hp, core, s_core, r_core)

    def to_far(d):
        return piece_copy(d, hp, far, s_y, r_y)

    def relay(d):
        return piece_copy(d, far, core, s_rel, r_rel)

    def each(lower, upper_, fn):
        def body(d, c):
            fn(d)
            return c

        lax.fori_loop(lower, upper_, body, 0)

    each(1, lists, lambda d: flag_copy(d).start())
    each(1, lists, lambda d: bucket_copy(d).start())
    recv[me, hp] = buckets[me]
    flags[hp, me] = flag_out[me]
    to_core(0).start()
    to_far(0).start()

    lane = iota((crows, n_rows), 1)
    row = iota((crows, n_rows), 0)
    label = jnp.concatenate([labels[k : k + 1, :] for k in range(list_dev)], axis=1)
    limit = jnp.zeros((1, n_rows), jnp.int32)
    lane1 = iota((1, n_rows), 1)
    for k in range(list_dev):
        inside = (lane1 >= k * rows) & (lane1 < (k + 1) * rows)
        limit = jnp.where(inside, sizes[k] + k * rows - hp * rows, limit)
    live_label = jnp.where(lane1 < limit, label, -1)
    half = jnp.zeros((crows, n_rows), F32)
    for k in range(list_dev):
        for a in range(2):
            pick = (row == 2 * k + a) & (lane >= k * rows) & (lane < (k + 1) * rows)
            half = jnp.where(pick & (live_label == a), 1.0, half)
    hb = half.astype(BF16)
    mine = dot(hb, hi) + dot(hb, lo)
    number = jnp.sum(half, axis=1, keepdims=True)
    parts[hp, :, 0:width] = mine
    parts[hp, :, width:] = jnp.broadcast_to(number, (crows, 128))

    for d in range(1, helps):
        help_copy(parts, s_part, r_part, d).start()

    for d in range(1, helps):
        help_copy(parts, s_part, r_part, d).wait_recv()
    summed = parts[0]
    for h in range(1, helps):
        summed = summed + parts[h]
    new_c = summed[:, 0:width] / jnp.maximum(summed[:, width : width + 1], 1.0)
    cents[me] = new_c
    each(1, lists, lambda d: cent_copy(d).start())

    each(1, lists, lambda d: flag_copy(d).wait_recv())
    for d in range(1, helps):
        help_copy(flags, s_fgat, r_fgat, d).start()
    for d in range(1, helps):
        help_copy(flags, s_fgat, r_fgat, d).wait_recv()
    for x in range(lists):
        for h in range(helps):
            flag_mat[x * helps + h : x * helps + h + 1, :] = flags[h, x]
    sources = lists * helps
    flag = flag_mat[...]
    before_lane = jnp.where(iota((128, 128), 0) < iota((128, 128), 1), 1.0, 0.0).astype(BF16)
    before_row = jnp.where(
        iota((sources, sources), 0) > iota((sources, sources), 1), 1.0, 0.0
    ).astype(BF16)
    ones = jnp.ones((128, 128), BF16)
    code = jnp.full((sources, 128), -1.0, F32)
    for k in range(list_dev):
        is_k = flag == float(k + 1)
        one_k = jnp.where(is_k, 1.0, 0.0).astype(BF16)
        place = dot(one_k, before_lane) + dot(before_row, dot(one_k, ones).astype(BF16))
        code = jnp.where(is_k, place + float(k * cap), code)
    spread = jnp.where(iota((sources, 128), 1) < depth, code, 0.0)
    step = depth
    while step < 128:
        spread = spread + pltpu.roll(spread, step, 1)
        step *= 2
    lane_h = iota((sources, 128), 1)
    row_h = lax.rem(iota((sources, 128), 0), helps)
    spread = jnp.where((lane_h >= row_h * depth) & (lane_h < (row_h + 1) * depth), spread, 0.0)
    for x in range(lists):
        codes[x] = jnp.sum(spread[x * helps : (x + 1) * helps, :], axis=0, keepdims=True)

    def ready(d):
        @pl.when(d > 0)
        def _():
            bucket_copy(d).wait_recv()
            to_core(d).start()
            to_far(d).start()

    def pass_on(d):
        to_far(d).wait_recv()
        relay(d).start()

    taken = helps * depth

    def place_pieces(steps, fresh):
        hots, terms = [], []
        for d in steps:
            to_core(d).wait_recv()
            relay(d).wait_recv()
            x = lax.rem(me + lists - hop(d), lists)
            put = codes[x][:, 0:taken].astype(jnp.int32)
            onehot = jnp.where(put == iota((list_dev * cap, taken), 0), 1.0, 0.0).astype(BF16)
            hots += [onehot, onehot]
            terms += split_parts(recv[x].reshape(taken, width))
        if taken % 128 == 0:
            moved = dot(jnp.concatenate(hots, axis=1), jnp.concatenate(terms, axis=0))
        else:
            moved = sum(dot(p, t) for p, t in zip(hots, terms))
        if fresh:
            out[...] = moved.reshape(list_dev, cap, width)
        else:
            out[...] += moved.reshape(list_dev, cap, width)

    def turn(t):
        d = 2 * t + 1
        ready(d)
        pass_on(d - 1)
        ready(d + 1)
        pass_on(d)
        place_pieces((d - 1, d), False)

    ready(1)
    pass_on(0)
    ready(2)
    pass_on(1)
    place_pieces((0, 1), True)
    each(1, lists // 2 - 1, turn)
    ready(lists - 1)
    pass_on(lists - 2)
    pass_on(lists - 1)

    each(1, lists, lambda d: cent_copy(d).wait_recv())
    n_c = lists * crows
    table[0:n_c, :] = cents[...].reshape(n_c, width)
    table[n_c:, :] = jnp.zeros((crows, width), F32)
    for k in range(list_dev):
        table[n_c + k : n_c + k + 1, :] = cent[k : k + 1, :]
    every = table[...]
    c_hi, c_lo = split_parts(every)
    cross = dot_t(c_hi, vhi[...]) + dot_t(c_hi, vlo[...]) + dot_t(c_lo, vhi[...])
    score = jnp.sum(every * every, axis=1, keepdims=True) - 2.0 * cross
    c_row = iota((n_c, rows), 0)
    in_block = lax.rem(c_row, crows)
    slot_of = jnp.where(
        in_block < 2 * list_dev,
        lax.div(c_row, crows) * list_dev + lax.div(in_block, 2),
        -1,
    )
    for k in range(list_dev):
        seen = jnp.zeros((n_c, rows), jnp.int32)
        touched = jnp.int32(0)
        for s in range(n_splits):
            at_slot = owner[split_ids[s]]
            hit = jnp.int32(0)
            for n in range(near):
                hit = jnp.maximum(
                    hit, jnp.where(owner[nearby[s, n]] == first + k, 1, 0).astype(jnp.int32)
                )
            touched = jnp.maximum(touched, hit)
            seen = jnp.maximum(seen, jnp.where(slot_of == at_slot, hit, 0))
        block = score[:, k * rows : (k + 1) * rows]
        best = jnp.min(jnp.where(seen > 0, block[0:n_c], 1e30), axis=0, keepdims=True)
        own = block[n_c + k : n_c + k + 1, :]
        top = jnp.where(touched > 0, sizes[k] - hp * rows, 0)
        ok = iota((1, rows), 1) < top
        gains[k : k + 1, :] = jnp.where(ok, (own - best) * (1.0 / width), 0.0)

    place_pieces((lists - 2, lists - 1), False)

    def drain(d):
        flag_copy(d).wait_send()
        bucket_copy(d).wait_send()
        cent_copy(d).wait_send()

    each(1, lists, drain)

    def drain_pieces(d):
        to_core(d).wait_send()
        to_far(d).wait_send()
        relay(d).wait_send()

    each(0, lists, drain_pieces)
    for d in range(1, helps):
        help_copy(parts, s_part, r_part, d).wait_send()
        help_copy(flags, s_fgat, r_fgat, d).wait_send()


def write_out(gains, arrived, gains_to, arrived_to, sems):
    rows = pltpu.make_async_copy(arrived, arrived_to, sems.at[0])
    few = pltpu.make_async_copy(gains, gains_to, sems.at[1])
    rows.start()
    few.start()
    few.wait()
    rows.wait()


def local(
    vectors, labels, list_sizes, centroids, split_ids, nearby, owner_map, mover_source, mover_dest
):
    list_dev, rows, width = vectors.shape
    lists = lax.axis_size("lists")
    helps = lax.axis_size("help")
    moves = mover_source.shape[0]
    most = max(2, (moves + lists - 1) // lists * 2)
    cap = lists * helps * ((most + list_dev - 1) // list_dev)
    depth = (most + 7) // 8 * 8
    crows = (2 * list_dev + 7) // 8 * 8
    vm = pl.BlockSpec(memory_space=pltpu.VMEM)
    sm = pl.BlockSpec(memory_space=pltpu.SMEM)
    sem = pltpu.SemaphoreType.DMA
    gains, arrived = pl.pallas_call(
        functools.partial(kernel, lists, helps, depth, cap, crows),
        out_shape=(
            pltpu.VMEM((list_dev, rows), F32),
            pltpu.VMEM((list_dev, cap, width), F32),
        ),
        in_specs=[vm] * 5 + [sm] * 4,
        out_specs=(vm, vm),
        scratch_shapes=[
            pltpu.VMEM((list_dev * rows, width), BF16),
            pltpu.VMEM((list_dev * rows, width), BF16),
            pltpu.VMEM((lists, depth, width), F32),
            pltpu.VMEM((lists, helps, depth, width), F32),
            pltpu.VMEM((lists, 1, 128), F32),
            pltpu.VMEM((helps, lists, 1, 128), F32),
            pltpu.VMEM((lists * helps, 128), F32),
            pltpu.VMEM((lists, 1, 128), F32),
            pltpu.VMEM((helps, crows, width + 128), F32),
            pltpu.VMEM((lists, crows, width), F32),
            pltpu.VMEM((lists * crows + crows, width), F32),
            sem((lists,)), sem((lists,)), sem((helps,)), sem((helps,)),
            sem((lists,)), sem((lists,)), sem((lists,)), sem((lists,)),
            sem((lists,)), sem((lists,)), sem((lists,)), sem((lists,)),
            sem((helps,)), sem((helps,)), sem((lists,)), sem((lists,)),
        ],
        compiler_params=pltpu.CompilerParams(
            collective_id=0, has_side_effects=True, vmem_limit_bytes=56 * 1024 * 1024
        ),
    )(
        vectors, labels, centroids, mover_source.reshape(1, moves), mover_dest.reshape(1, moves),
        list_sizes, split_ids, nearby, owner_map,
    )
    hbm = pl.BlockSpec(memory_space=pl.ANY)
    return pl.pallas_call(
        write_out,
        out_shape=(
            jax.ShapeDtypeStruct((list_dev, rows), F32),
            jax.ShapeDtypeStruct((list_dev, cap, width), F32),
        ),
        in_specs=[vm, vm],
        out_specs=(hbm, hbm),
        scratch_shapes=[sem((2,))],
        compiler_params=pltpu.CompilerParams(vmem_limit_bytes=8 * 1024 * 1024),
    )(gains, arrived)


def solution(mesh):
    in_specs = (
        P("lists", "help", None),
        P("lists", "help"),
        P("lists"),
        P("lists", None),
        P(),
        P(),
        P(),
        P(("lists", "help")),
        P(("lists", "help")),
    )
    out_specs = (P("lists", "help"), P("lists", None, None))
    return jax.shard_map(local, mesh=mesh, in_specs=in_specs, out_specs=out_specs, check_vma=False)
```
